32 devices in a mesh: grp: 2 (over x), len: 16 (over z, y, core).
Axes of the slice: x: 2, y: 2, z: 4, core: 2. Of those that a mesh axis runs over, the one named last changes fastest.
Arguments:
- tin_temp: float32 [64, 512, 1024], P(None, ('grp', 'len')), parts along dimension 1, may hold values from -6 to 6
- flow_code: int32 [64, 512, 1024], P(None, ('grp', 'len')), parts along dimension 1, may hold values from 0 to 3
- speeds: float32 [2, 64], replicated, may hold values from 0.02 to 0.12
- floor_temp: float32 [32, 48, 64, 256], P(('grp', 'len')), parts along dimension 0, may hold values from -6 to 6
- material: int32 [32, 48, 64, 256], P(('grp', 'len')), parts along dimension 0, may hold values from 0 to 2
- conductivity: float32 [3], replicated, may hold values from 0.03 to 0.15
Outputs:
- tin_out: float32 [64, 512, 1024], P(None, ('grp', 'len')), parts along dimension 1
- floor_out: float32 [32, 48, 64, 256], P(('grp', 'len')), parts along dimension 0
The draws below stay inside these ranges and needn't reach their ends.
There are 2 independent parts, one for each index of `grp`. The reference program is written for one: setup_inputs(seed, part) draws one part's arguments, and reference() takes and returns one part's arrays. A program takes and returns all parts, laid end to end along the dimension named above; an argument that names none is the same for every part. Nothing has to cross between parts.
Inputs may be any that keep to these rules, and one draw needn't show every extreme that they name: flow_code % 2 is 0 where the tin cell takes its length upwind value from the lower length index and 1 from the higher; flow_code // 2 likewise across the width. material ids index conductivity.
All inputs are finite; a program needn't handle non-finite values.
Results may differ from the reference program's by a relative error of at most 0.0003.
Values sent between devices are 32-bit elements; how exact they have to be, the bound alone decides.
A program may use at most 128 MiB of HBM per device.

```python
import jax
import jax.numpy as jnp

NY = 1024
ZT = 64
ZR = 48
TILE_Y = 4
MATS = 3
SWEEPS = 2
NX = 256
TILE_X = 4
CXR = 64
CYR = 256
N_LEN = 16


def plant(drawn, own_key, least, high):
    place = [jax.random.randint(jax.random.fold_in(own_key, axis), (), 0, length) for axis, length in enumerate(drawn.shape)]
    longest = drawn.shape.index(max(drawn.shape))
    neighbour = place[:longest] + [(place[longest] + 1) % drawn.shape[longest]] + place[longest + 1:]
    return drawn.at[tuple(place)].set(least).at[tuple(neighbour)].set(high)


def levels(rng, dims, cuts, least, top_value):
    factor_of = 1.0
    for axis_at, blocks in cuts:
        draws = jax.random.uniform(jax.random.fold_in(jax.random.fold_in(rng, 6), axis_at), (blocks,), jnp.float32, least / len(cuts), top_value / len(cuts))
        factor_of = factor_of * jnp.repeat(jnp.exp(draws), dims[axis_at] // blocks).reshape((-1,) + (1,) * (len(dims) - 1 - axis_at))
    return factor_of


def scatter_about(own_key, shape, deviation, limit, cuts=(), dtype=jnp.bfloat16):
    values = deviation * jax.random.normal(own_key, shape, jnp.float32)
    if cuts:
        values = values * levels(own_key, shape, cuts, -0.22, 0.18)
    return jnp.clip(values, -limit, limit).astype(dtype)


def setup_inputs(seed: int = 0, part: int = 0) -> dict:
    seeds = jax.random.split(jax.random.key(seed), 7)
    part_keys = jax.random.split(jax.random.fold_in(seeds[6], part), 7)
    tin_temp = scatter_about(part_keys[0], (ZT, NX, NY), 1.0, 6.0, ((1, 16),), jnp.float32)
    flow_code = plant(jax.random.randint(part_keys[1], (ZT, NX, NY), 0, 4), jax.random.fold_in(part_keys[1], 1), 0, 3).astype(jnp.int32)
    speeds = jnp.clip(jax.random.uniform(seeds[2], (2, ZT), jnp.float32, 0.02, 0.12), 0.02, 0.12)
    floor_temp = scatter_about(part_keys[3], (N_LEN, ZR, CXR, CYR), 1.0, 6.0, ((0, 16),), jnp.float32)
    material = plant(jax.random.randint(part_keys[4], (N_LEN, ZR, CXR, CYR), 0, MATS), jax.random.fold_in(part_keys[4], 1), 0, MATS - 1).astype(jnp.int32)
    conductivity = jnp.clip(jax.random.uniform(seeds[5], (MATS,), jnp.float32, 0.03, 0.15), 0.03, 0.15)
    return {"tin_temp": tin_temp, "flow_code": flow_code, "speeds": speeds, "floor_temp": floor_temp, "material": material, "conductivity": conductivity}


KT = 0.1
HT = 0.2
HR = 0.2


def lookup(material, conductivity):
    result = jnp.zeros(material.shape, jnp.float32)
    for material_id in range(conductivity.shape[0]):
        result = result + jnp.where(material == material_id, conductivity[material_id], 0.0)
    return result


def tin_update(tin_field, padded, flow_code, speeds, top_plane):
    x_minus = padded[:, :-2, 1:-1]
    x_plus = padded[:, 2:, 1:-1]
    y_minus = padded[:, 1:-1, :-2]
    y_plus = padded[:, 1:-1, 2:]
    layer_above = jnp.concatenate([tin_field[1:], tin_field[-1:]], 0)
    layer_below = jnp.concatenate([tin_field[:1], tin_field[:-1]], 0)
    spread = x_minus + x_plus + y_minus + y_plus + layer_above + layer_below - 6.0 * tin_field
    speed_x = speeds[0][:, None, None]
    speed_y = speeds[1][:, None, None]
    carried = jnp.where(flow_code % 2 == 0, speed_x * (x_minus - tin_field), speed_x * (x_plus - tin_field))
    carried = carried + jnp.where(flow_code // 2 == 0, speed_y * (y_minus - tin_field), speed_y * (y_plus - tin_field))
    layer_ids = jnp.arange(tin_field.shape[0])[:, None, None]
    contact = jnp.where(layer_ids == 0, HT * (top_plane[None] - tin_field[0:1]), 0.0)
    return tin_field + KT * spread + carried + contact


def floor_update(floor_field, conduct, along_x, conduct_x, along_y, conduct_y, bottom_tin):
    lateral = 0.5 * (conduct + conduct_x[:, :-2]) * (along_x[:, :-2] - floor_field)
    lateral = lateral + 0.5 * (conduct + conduct_x[:, 2:]) * (along_x[:, 2:] - floor_field)
    lateral = lateral + 0.5 * (conduct + conduct_y[:, :, :-2]) * (along_y[:, :, :-2] - floor_field)
    lateral = lateral + 0.5 * (conduct + conduct_y[:, :, 2:]) * (along_y[:, :, 2:] - floor_field)
    field_above = jnp.concatenate([floor_field[:1], floor_field[:-1]], 0)
    conduct_above = jnp.concatenate([conduct[:1], conduct[:-1]], 0)
    field_below = jnp.concatenate([floor_field[1:], jnp.zeros_like(floor_field[:1])], 0)
    conduct_below = jnp.concatenate([conduct[1:], jnp.zeros_like(conduct[:1])], 0)
    vertical = 0.5 * (conduct + conduct_above) * (field_above - floor_field)
    vertical = vertical + 0.5 * (conduct + conduct_below) * (field_below - floor_field)
    layer_ids = jnp.arange(floor_field.shape[0])[:, None, None]
    contact = jnp.where(layer_ids == 0, HR * (bottom_tin[None] - floor_field[0:1]), 0.0)
    return floor_field + lateral + vertical + contact


def to_grid(tile_array):
    shaped = tile_array.reshape(TILE_X, TILE_Y, ZR, CXR, CYR)
    return shaped.transpose(2, 0, 3, 1, 4).reshape(ZR, NX, NY)


def to_tiles(grid_array):
    shaped = grid_array.reshape(ZR, TILE_X, CXR, TILE_Y, CYR)
    return shaped.transpose(1, 3, 0, 2, 4).reshape(N_LEN, ZR, CXR, CYR)


def reference(tin_temp, flow_code, speeds, floor_temp, material, conductivity):
    tin_field = tin_temp
    floor_field = to_grid(floor_temp)
    conduct = lookup(to_grid(material), conductivity)
    pad_x = ((0, 0), (1, 1), (0, 0))
    pad_y = ((0, 0), (0, 0), (1, 1))
    conduct_x = jnp.pad(conduct, pad_x)
    conduct_y = jnp.pad(conduct, pad_y)
    for repeat in range(SWEEPS):
        bottom_tin = tin_field[0]
        top_plane = floor_field[0]
        padded = jnp.pad(tin_field, ((0, 0), (1, 1), (1, 1)))
        tin_next = tin_update(tin_field, padded, flow_code, speeds, top_plane)
        floor_next = floor_update(floor_field, conduct, jnp.pad(floor_field, pad_x), conduct_x,
                                  jnp.pad(floor_field, pad_y), conduct_y, bottom_tin)
        tin_field = tin_next
        floor_field = floor_next
    return tin_field, to_tiles(floor_field)
```

```python
import functools

import jax
import jax.numpy as jnp
from jax import lax
from jax.experimental import pallas as pl
from jax.experimental.pallas import tpu as pltpu
from jax.sharding import PartitionSpec as P

KT = 0.1
HT = 0.2
HR = 0.2
L = 128
S = 8


def kernel(n, ty, tin_h, flow_h, speeds, floor_h, mat_h, cond,
           tin_o, floor_o,
           tin0, flow, tin1, floor0, mat, floor1, kh, kx, ky, kz,
           tlo, thi, tlo_s, thi_s,
           rlo, rhi, rlo_s, rhi_s,
           clo, chi, clo_s, chi_s,
           pp, bb, load_sem, send_sem, recv_sem):
    Z, R, NYW = tin_h.shape
    ZF, CX, CY = floor_h.shape
    me = lax.axis_index("len")
    c = lax.rem(me, ty)
    base = me - c
    up_ok, dn_ok = me < n - 1, me > 0
    rup_ok, rdn_ok = me + ty < n, me >= ty
    cup_ok, cdn_ok = c < ty - 1, c > 0

    loads = [pltpu.make_async_copy(a, b, load_sem.at[i]) for i, (a, b) in enumerate(
        [(tin_h, tin0), (mat_h, mat), (floor_h, floor0), (flow_h, flow)])]
    for ld in loads:
        ld.start()

    barrier = pltpu.get_barrier_semaphore()

    def hello(target):
        pl.semaphore_signal(barrier, inc=1, device_id={"len": target},
                            device_id_type=pl.DeviceIdType.MESH)

    for d in range(1, ty):
        hello(base + lax.rem(c + d, ty))
    pairs = [(rup_ok, me + ty), (rdn_ok, me - ty),
             (jnp.logical_and(c == ty - 1, up_ok), me + 1),
             (jnp.logical_and(c == 0, dn_ok), me - 1)]
    for ok, target in pairs:
        @pl.when(ok)
        def _():
            hello(target)

    row = lax.broadcasted_iota(jnp.int32, (S, L), 0)
    lane = lax.broadcasted_iota(jnp.int32, (S, L), 1)
    row_first, row_last = row == 0, row == S - 1
    lane_first, lane_last = lane == 0, lane == L - 1

    own_p = pltpu.make_async_copy(
        floor_h.at[0, pl.ds(pl.multiple_of(c * R, R), R), :],
        pp.at[0, :, pl.ds(pl.multiple_of(c * CY, CY), CY)], load_sem.at[4])
    own_b = pltpu.make_async_copy(
        tin_h.at[0, :, pl.ds(pl.multiple_of(c * CY, CY), CY)],
        bb.at[0, pl.ds(pl.multiple_of(c * R, R), R), :], load_sem.at[5])
    own_p.start()
    own_b.start()

    def remote(e, slot, src, dst, target):
        return pltpu.make_async_remote_copy(
            src_ref=src, dst_ref=dst, send_sem=send_sem.at[e, slot],
            recv_sem=recv_sem.at[e, slot], device_id={"len": target},
            device_id_type=pl.DeviceIdType.MESH)

    def tin_msgs(e):
        return [(up_ok, dn_ok, remote(e, 0, thi_s.at[e], tlo.at[e], me + 1), tlo),
                (dn_ok, up_ok, remote(e, 1, tlo_s.at[e], thi.at[e], me - 1), thi)]

    def floor_msgs(e):
        if e == 0:
            return [
                (rup_ok, rdn_ok, remote(0, 2, rhi_s.at[0:2], rlo.at[0:2], me + ty), rlo),
                (rdn_ok, rup_ok, remote(0, 3, rlo_s.at[0:2], rhi.at[0:2], me - ty), rhi),
                (cup_ok, cdn_ok, remote(0, 4, chi_s.at[0:2], clo.at[0:2], me + 1), clo),
                (cdn_ok, cup_ok, remote(0, 5, clo_s.at[0:2], chi.at[0:2], me - 1), chi)]
        return [
            (rup_ok, rdn_ok, remote(1, 2, rhi_s.at[2], rlo.at[2], me + ty), rlo),
            (rdn_ok, rup_ok, remote(1, 3, rlo_s.at[2], rhi.at[2], me - ty), rhi),
            (cup_ok, cdn_ok, remote(1, 4, chi_s.at[2], clo.at[2], me + 1), clo),
            (cdn_ok, cup_ok, remote(1, 5, clo_s.at[2], chi.at[2], me - 1), chi)]

    def p_msgs(e, field):
        out = []
        for d in range(1, ty):
            t = lax.rem(c + d, ty)
            out.append(remote(
                e, 5 + d, field.at[0, pl.ds(pl.multiple_of(t * R, R), R), :],
                pp.at[e, :, pl.ds(pl.multiple_of(c * CY, CY), CY)], base + t))
        return out

    def b_msgs(e, field):
        out = []
        for d in range(1, ty):
            t = lax.rem(c + d, ty)
            out.append(remote(
                e, 8 + d, field.at[0, :, pl.ds(pl.multiple_of(t * CY, CY), CY)],
                bb.at[e, pl.ds(pl.multiple_of(c * R, R), R), :], base + t))
        return out

    def start_if(msgs):
        for ok, _, m, _ in msgs:
            @pl.when(ok)
            def _():
                m.start()

    def wait_recv_if(msgs):
        for _, ok, m, _ in msgs:
            @pl.when(ok)
            def _():
                m.wait_recv()

    def wait_send_if(msgs):
        for ok, _, m, _ in msgs:
            @pl.when(ok)
            def _():
                m.wait_send()

    def tile(ref, z, i, j):
        return ref[z, pl.ds(i * S, S), pl.ds(j * L, L)]

    for _, ok, _, buf in tin_msgs(0) + floor_msgs(0):
        @pl.when(jnp.logical_not(ok))
        def _():
            buf[...] = jnp.zeros_like(buf)

    loads[0].wait()

    def pack_tin(z, carry):
        tlo_s[0, pl.ds(z, 1), :] = tin0[z, 0:1, :]
        thi_s[0, pl.ds(z, 1), :] = tin0[z, R - 1:R, :]
        return carry

    lax.fori_loop(0, Z, pack_tin, 0, unroll=4)

    peers = ty - 1
    for ok, _ in pairs:
        peers = peers + ok.astype(jnp.int32)
    pl.semaphore_wait(barrier, peers)

    t0, f0 = tin_msgs(0), floor_msgs(0)
    p0, b0 = p_msgs(0, floor_h), b_msgs(0, tin_h)
    start_if(t0)
    for m in b0 + p0:
        m.start()

    loads[1].wait()
    c0, c1, c2 = cond[0] * 0.5, cond[1] * 0.5, cond[2] * 0.5
    NI, NJ = CX // S, CY // L

    def pack_cols(z, edge_lo, edge_hi, acc):
        lo_acc, hi_acc = acc
        here = lane == z
        lo_n = tuple(jnp.where(here, pltpu.roll(edge_lo[i], z, 1), lo_acc[i]) for i in range(NI))
        hi_n = tuple(jnp.where(here, pltpu.roll(edge_hi[i], z + 1, 1), hi_acc[i]) for i in range(NI))
        return lo_n, hi_n

    def zeros():
        zero = jnp.zeros((S, L), jnp.float32)
        return tuple(zero for _ in range(NI)), tuple(zero for _ in range(NI))

    def store_cols(slot, acc):
        for i in range(NI):
            clo_s[slot, pl.ds(i * S, S), :] = acc[0][i]
            chi_s[slot, pl.ds(i * S, S), :] = acc[1][i]

    def k_layer(z, acc):
        t = {}
        for i in range(NI):
            for j in range(NJ):
                m = tile(mat, z, i, j)
                v = jnp.where(m == 0, c0, jnp.where(m == 1, c1, c2))
                kh[z, pl.ds(i * S, S), pl.ds(j * L, L)] = v
                t[i, j] = v
        rlo_s[1, pl.ds(z, 1), :] = jnp.concatenate([t[0, j][0:1] for j in range(NJ)], 1)
        rhi_s[1, pl.ds(z, 1), :] = jnp.concatenate([t[NI - 1, j][S - 1:S] for j in range(NJ)], 1)
        return pack_cols(z, [t[i, 0] for i in range(NI)], [t[i, NJ - 1] for i in range(NI)], acc)

    store_cols(1, lax.fori_loop(0, ZF, k_layer, zeros()))
    loads[2].wait()

    def g_layer(z, acc):
        rlo_s[0, pl.ds(z, 1), :] = floor0[z, 0:1, :]
        rhi_s[0, pl.ds(z, 1), :] = floor0[z, CX - 1:CX, :]
        return pack_cols(z, [tile(floor0, z, i, 0) for i in range(NI)],
                         [tile(floor0, z, i, NJ - 1) for i in range(NI)], acc)

    store_cols(0, lax.fori_loop(0, ZF, g_layer, zeros()))
    start_if(f0)

    def floor_layer(first, src, dst, z, top, bottom):
        g, kxt, kyt = {}, {}, {}
        span = [(i, j) for i in range(NI) for j in range(NJ)]
        for i, j in span:
            g[i, j] = tile(src, z, i, j)
        if first:
            k = {ij: tile(kh, z, *ij) for ij in span}
            for i, j in span:
                r = pltpu.roll(k[i, j], S - 1, 0)
                if i < NI - 1:
                    v = k[i, j] + jnp.where(row_last, pltpu.roll(k[i + 1, j], S - 1, 0), r)
                else:
                    v = jnp.where(row_last, 0.0, k[i, j] + r)
                kxt[i, j] = v
                kx[z, pl.ds(i * S, S), pl.ds(j * L, L)] = v
                r = pltpu.roll(k[i, j], L - 1, 1)
                if j < NJ - 1:
                    v = k[i, j] + jnp.where(lane_last, pltpu.roll(k[i, j + 1], L - 1, 1), r)
                else:
                    v = jnp.where(lane_last, 0.0, k[i, j] + r)
                kyt[i, j] = v
                ky[z, pl.ds(i * S, S), pl.ds(j * L, L)] = v
                if bottom:
                    v = k[i, j]
                else:
                    v = k[i, j] + tile(kh, z + 1, i, j)
                kz[z, pl.ds(i * S, S), pl.ds(j * L, L)] = v
        else:
            for i, j in span:
                kxt[i, j] = tile(kx, z, i, j)
                kyt[i, j] = tile(ky, z, i, j)
        rx = {ij: pltpu.roll(g[ij], S - 1, 0) for ij in span}
        ry = {ij: pltpu.roll(g[ij], L - 1, 1) for ij in span}
        fx, fy, sx, sy = {}, {}, {}, {}
        for i, j in span:
            nx = rx[i, j] if i == NI - 1 else jnp.where(row_last, rx[i + 1, j], rx[i, j])
            ny = ry[i, j] if j == NJ - 1 else jnp.where(lane_last, ry[i, j + 1], ry[i, j])
            fx[i, j] = kxt[i, j] * (nx - g[i, j])
            fy[i, j] = kyt[i, j] * (ny - g[i, j])
            sx[i, j] = pltpu.roll(fx[i, j], 1, 0)
            sy[i, j] = pltpu.roll(fy[i, j], 1, 1)
        for i, j in span:
            px = jnp.where(row_first, sx[(i - 1) % NI, j], sx[i, j])
            py = jnp.where(lane_first, sy[i, (j - 1) % NJ], sy[i, j])
            if bottom:
                down = tile(kz, z, i, j) * g[i, j]
                new = g[i, j] - down
            else:
                new = g[i, j] + tile(kz, z, i, j) * (tile(src, z + 1, i, j) - g[i, j])
            if not top:
                new = new - tile(kz, z - 1, i, j) * (g[i, j] - tile(src, z - 1, i, j))
            new = new + ((fx[i, j] - px) + (fy[i, j] - py))
            dst[z, pl.ds(i * S, S), pl.ds(j * L, L)] = new

    def floor_sweep(first, src, dst):
        floor_layer(first, src, dst, 0, True, False)

        def body(z, carry):
            floor_layer(first, src, dst, z, False, False)
            return carry

        lax.fori_loop(1, ZF - 1, body, 0)
        floor_layer(first, src, dst, ZF - 1, False, True)

    def floor_edges(e, src, dst):
        g = 2 * e
        slot = 0 if e == 0 else 2
        rlo[slot] = (rlo_s[1] + rlo[1]) * (rlo[slot] - rlo_s[slot])
        rhi[slot] = (rhi_s[1] + rhi[1]) * (rhi[slot] - rhi_s[slot])
        clo[slot] = (clo_s[1] + clo[1]) * (clo[slot] - clo_s[slot])
        chi[slot] = (chi_s[1] + chi[1]) * (chi[slot] - chi_s[slot])
        dst[0] = dst[0] + HR * (bb[e] - src[0])

        def body(z, acc):
            row_lo, row_hi = rlo[slot, pl.ds(z, 1), :], rhi[slot, pl.ds(z, 1), :]
            t = {(i, j): tile(dst, z, i, j) for i in range(NI) for j in range(NJ)}
            for j in range(NJ):
                t[0, j] = t[0, j] + jnp.where(row_first, row_lo[:, j * L:j * L + L], 0.0)
                t[NI - 1, j] = t[NI - 1, j] + jnp.where(
                    row_last, row_hi[:, j * L:j * L + L], 0.0)
            for i in range(NI):
                low = pltpu.roll(clo[slot, pl.ds(i * S, S), :], lax.rem(L - z, L), 1)
                high = pltpu.roll(chi[slot, pl.ds(i * S, S), :], L - 1 - z, 1)
                t[i, 0] = t[i, 0] + jnp.where(lane_first, low, 0.0)
                t[i, NJ - 1] = t[i, NJ - 1] + jnp.where(lane_last, high, 0.0)
            for (i, j), v in t.items():
                dst[z, pl.ds(i * S, S), pl.ds(j * L, L)] = v
            if e == 1:
                return acc
            rlo_s[2, pl.ds(z, 1), :] = jnp.concatenate([t[0, j][0:1] for j in range(NJ)], 1)
            rhi_s[2, pl.ds(z, 1), :] = jnp.concatenate([t[NI - 1, j][S - 1:S] for j in range(NJ)], 1)
            return pack_cols(z, [t[i, 0] for i in range(NI)],
                             [t[i, NJ - 1] for i in range(NI)], acc)

        if e == 0:
            store_cols(2, lax.fori_loop(0, ZF, body, zeros()))
        else:
            lax.fori_loop(0, ZF, body, 0)

    NH, NK = R // S, NYW // L

    def tin_layer(e, src, dst, z, zu, zd, top):
        span = [(h, k) for h in range(NH) for k in range(NK)]
        s_x, s_y = speeds[0, z], speeds[1, z]
        keep = (1.0 - 6.0 * KT) - s_x - s_y
        u = {hk: tile(src, z, *hk) for hk in span}
        rd = {hk: pltpu.roll(u[hk], 1, 0) for hk in span}
        ru = {hk: pltpu.roll(u[hk], S - 1, 0) for hk in span}
        ld = {hk: pltpu.roll(u[hk], 1, 1) for hk in span}
        lu = {hk: pltpu.roll(u[hk], L - 1, 1) for hk in span}
        first_row, last_row = [], []
        before, after = tlo[e, pl.ds(z, 1), :], thi[e, pl.ds(z, 1), :]
        for h, k in span:
            v = u[h, k]
            below = before[:, k * L:k * L + L] if h == 0 else rd[h - 1, k]
            above = after[:, k * L:k * L + L] if h == NH - 1 else ru[h + 1, k]
            xm = jnp.where(row_first, below, rd[h, k])
            xp = jnp.where(row_last, above, ru[h, k])
            ym = jnp.where(lane_first, 0.0 if k == 0 else ld[h, k - 1], ld[h, k])
            yp = jnp.where(lane_last, 0.0 if k == NK - 1 else lu[h, k + 1], lu[h, k])
            f = tile(flow, z, h, k)
            total = ((xm + xp) + (ym + yp)) + (tile(src, zu, h, k) + tile(src, zd, h, k))
            new = keep * v + KT * total
            new = new + s_x * jnp.where((f & 1) == 0, xm, xp)
            new = new + s_y * jnp.where(f < 2, ym, yp)
            if top:
                new = new + HT * (pp[e, pl.ds(h * S, S), pl.ds(k * L, L)] - v)
            dst[z, pl.ds(h * S, S), pl.ds(k * L, L)] = new
            if h == 0:
                first_row.append(new[0:1])
            if h == NH - 1:
                last_row.append(new[S - 1:S])
        if e == 0:
            tlo_s[1, pl.ds(z, 1), :] = jnp.concatenate(first_row, 1)
            thi_s[1, pl.ds(z, 1), :] = jnp.concatenate(last_row, 1)

    def tin_sweep(e, src, dst):
        tin_layer(e, src, dst, 0, 1, 0, True)

        def body(z, carry):
            tin_layer(e, src, dst, z, jnp.minimum(z + 1, Z - 1), z - 1, False)
            return carry

        lax.fori_loop(1, Z, body, 0)

    floor_sweep(True, floor0, floor1)
    wait_recv_if(f0)
    for m in b0:
        m.wait_recv()
    own_b.wait()
    wait_send_if(f0)
    floor_edges(0, floor0, floor1)
    f1, p1 = floor_msgs(1), p_msgs(1, floor1)
    start_if(f1)
    for m in p1:
        m.start()
    own_p1 = pltpu.make_async_copy(
        floor1.at[0, pl.ds(pl.multiple_of(c * R, R), R), :],
        pp.at[1, :, pl.ds(pl.multiple_of(c * CY, CY), CY)], load_sem.at[6])
    own_p1.start()

    loads[3].wait()
    wait_recv_if(t0)
    for m in p0:
        m.wait_recv()
    own_p.wait()
    tin_sweep(0, tin0, tin1)
    t1, b1 = tin_msgs(1), b_msgs(1, tin1)
    start_if(t1)
    for m in b1:
        m.start()
    own_b1 = pltpu.make_async_copy(
        tin1.at[0, :, pl.ds(pl.multiple_of(c * CY, CY), CY)],
        bb.at[1, pl.ds(pl.multiple_of(c * R, R), R), :], load_sem.at[7])
    own_b1.start()

    floor_sweep(False, floor1, floor_o)
    wait_recv_if(f1)
    for m in b1:
        m.wait_recv()
    own_b1.wait()
    wait_send_if(f1)
    floor_edges(1, floor1, floor_o)

    wait_recv_if(t1)
    for m in p1:
        m.wait_recv()
    own_p1.wait()
    tin_sweep(1, tin1, tin_o)

    wait_send_if(t0)
    wait_send_if(t1)
    for m in p0 + b0 + p1 + b1:
        m.wait_send()


def local(n, ty, tin_temp, flow_code, speeds, floor_temp, material, conductivity):
    tin_shape = tin_temp.shape
    floor_shape = floor_temp.shape[1:]
    Z, R, NYW = tin_shape
    ZF, CX, CY = floor_shape
    f32, i32 = jnp.float32, jnp.int32
    V = pltpu.VMEM
    tin_v, floor_v = V(tin_shape, f32), V(floor_shape, f32)
    edge_t = V((2, Z, NYW), f32)
    edge_r = V((3, ZF, CY), f32)
    edge_c = V((3, CX, L), f32)
    tin_out, floor_out = pl.pallas_call(
        functools.partial(kernel, n, ty),
        out_shape=OUT(tin_shape, floor_shape),
        in_specs=[pl.BlockSpec(memory_space=m) for m in
                  (pl.ANY, pl.ANY, pltpu.SMEM, pl.ANY, pl.ANY, pltpu.SMEM)],
        out_specs=[pl.BlockSpec(memory_space=pltpu.VMEM)] * 2,
        scratch_shapes=[
            tin_v, V(tin_shape, i32), tin_v, floor_v, V(floor_shape, i32), floor_v,
            floor_v, floor_v, floor_v, floor_v,
            edge_t, edge_t, edge_t, edge_t,
            edge_r, edge_r, edge_r, edge_r,
            edge_c, edge_c, edge_c, edge_c,
            V((2, R, NYW), f32), V((2, CX, CY), f32),
            pltpu.SemaphoreType.DMA((8,)),
            pltpu.SemaphoreType.DMA((2, 12)),
            pltpu.SemaphoreType.DMA((2, 12)),
        ],
        compiler_params=pltpu.CompilerParams(
            collective_id=0, has_side_effects=True, vmem_limit_bytes=52 * 1024 * 1024),
        cost_estimate=pl.CostEstimate(flops=120_000_000, bytes_accessed=23_000_000, transcendentals=0),
    )(tin_temp, flow_code, speeds, floor_temp[0], material[0], conductivity)
    return tin_out, floor_out[None]


def OUT(tin_shape, floor_shape):
    return [jax.ShapeDtypeStruct(tin_shape, jnp.float32),
            jax.ShapeDtypeStruct(floor_shape, jnp.float32)]


def solution(mesh):
    n = mesh.shape["len"]
    split = ("grp", "len")
    placed = (P(None, split, None), P(None, split, None), P(),
              P(split, None, None, None), P(split, None, None, None), P())

    def whole(tin_temp, flow_code, speeds, floor_temp, material, conductivity):
        ty = tin_temp.shape[2] // floor_temp.shape[3]
        return jax.shard_map(
            functools.partial(local, n, ty),
            mesh=mesh,
            in_specs=placed,
            out_specs=(P(None, split, None), P(split, None, None, None)),
            check_vma=False,
        )(tin_temp, flow_code, speeds, floor_temp, material, conductivity)

    return whole
```

```python
import functools

import jax
import jax.numpy as jnp
from jax import lax
from jax.experimental import pallas as pl
from jax.experimental.pallas import tpu as pltpu
from jax.sharding import PartitionSpec as P

KT = 0.1
HT = 0.2
HR = 0.2
L = 128
NQ = 4
S = 8


def kernel(n, ty, tin_h, flow_h, speeds_h, floor_h, mat_h, cond_h,
           tin_o, floor_o,
           speeds, cond, tin0, flow, tin1, floor0, mat, floor1, kh, kx, ky, kz,
           tlo, thi, tlo_s, thi_s,
           rlo, rhi, rlo_s, rhi_s,
           clo, chi, clo_s, chi_s,
           pp, bb, load_sem, send_sem, recv_sem):
    Z, R, NYW = tin_h.shape
    ZF, CX, CY = floor_h.shape
    me = lax.axis_index("len")
    c = lax.rem(me, ty)
    base = me - c
    up_ok, dn_ok = me < n - 1, me > 0
    rup_ok, rdn_ok = me + ty < n, me >= ty
    cup_ok, cdn_ok = c < ty - 1, c > 0

    loads = [pltpu.make_async_copy(a, b, load_sem.at[i]) for i, (a, b) in enumerate(
        [(tin_h, tin0), (mat_h, mat), (floor_h, floor0), (flow_h, flow)])]
    scalars = [pltpu.make_async_copy(cond_h, cond, load_sem.at[8]),
               pltpu.make_async_copy(speeds_h, speeds, load_sem.at[9])]
    for ld in scalars:
        ld.start()
    for ld in loads:
        ld.start()

    barrier = pltpu.get_barrier_semaphore()

    def hello(target):
        pl.semaphore_signal(barrier, inc=1, device_id={"len": target},
                            device_id_type=pl.DeviceIdType.MESH)

    for d in range(1, ty):
        hello(base + lax.rem(c + d, ty))
    pairs = [(rup_ok, me + ty), (rdn_ok, me - ty),
             (jnp.logical_and(c == ty - 1, up_ok), me + 1),
             (jnp.logical_and(c == 0, dn_ok), me - 1)]
    for ok, target in pairs:
        @pl.when(ok)
        def _():
            hello(target)

    row = lax.broadcasted_iota(jnp.int32, (S, L), 0)
    lane = lax.broadcasted_iota(jnp.int32, (S, L), 1)
    row_first, row_last = row == 0, row == S - 1
    lane_first, lane_last = lane == 0, lane == L - 1

    own_p = pltpu.make_async_copy(
        floor_h.at[0, pl.ds(pl.multiple_of(c * R, R), R), :],
        pp.at[0, :, pl.ds(pl.multiple_of(c * CY, CY), CY)], load_sem.at[4])
    own_b = pltpu.make_async_copy(
        tin_h.at[0, :, pl.ds(pl.multiple_of(c * CY, CY), CY)],
        bb.at[0, pl.ds(pl.multiple_of(c * R, R), R), :], load_sem.at[5])
    own_p.start()
    own_b.start()

    def remote(e, slot, src, dst, target):
        return pltpu.make_async_remote_copy(
            src_ref=src, dst_ref=dst, send_sem=send_sem.at[e, slot],
            recv_sem=recv_sem.at[e, slot], device_id={"len": target},
            device_id_type=pl.DeviceIdType.MESH)

    ZQ = Z // NQ

    def tin_msgs(e, q):
        part = pl.ds(q * ZQ, ZQ)
        return [(up_ok, dn_ok, remote(e, 12 + q, thi_s.at[e, part], tlo.at[e, part], me + 1), tlo),
                (dn_ok, up_ok, remote(e, 12 + NQ + q, tlo_s.at[e, part], thi.at[e, part], me - 1), thi)]

    def floor_msgs(e):
        if e == 0:
            return [
                (rup_ok, rdn_ok, remote(0, 2, rhi_s.at[0:2], rlo.at[0:2], me + ty), rlo),
                (rdn_ok, rup_ok, remote(0, 3, rlo_s.at[0:2], rhi.at[0:2], me - ty), rhi),
                (cup_ok, cdn_ok, remote(0, 4, chi_s.at[0:2], clo.at[0:2], me + 1), clo),
                (cdn_ok, cup_ok, remote(0, 5, clo_s.at[0:2], chi.at[0:2], me - 1), chi)]
        return [
            (rup_ok, rdn_ok, remote(1, 2, rhi_s.at[2], rlo.at[2], me + ty), rlo),
            (rdn_ok, rup_ok, remote(1, 3, rlo_s.at[2], rhi.at[2], me - ty), rhi),
            (cup_ok, cdn_ok, remote(1, 4, chi_s.at[2], clo.at[2], me + 1), clo),
            (cdn_ok, cup_ok, remote(1, 5, clo_s.at[2], chi.at[2], me - 1), chi)]

    def p_msgs(e, field):
        out = []
        for d in range(1, ty):
            t = lax.rem(c + d, ty)
            out.append(remote(
                e, 5 + d, field.at[0, pl.ds(pl.multiple_of(t * R, R), R), :],
                pp.at[e, :, pl.ds(pl.multiple_of(c * CY, CY), CY)], base + t))
        return out

    def b_msgs(e, field):
        out = []
        for d in range(1, ty):
            t = lax.rem(c + d, ty)
            out.append(remote(
                e, 8 + d, field.at[0, :, pl.ds(pl.multiple_of(t * CY, CY), CY)],
                bb.at[e, pl.ds(pl.multiple_of(c * R, R), R), :], base + t))
        return out

    def start_if(msgs):
        for ok, _, m, _ in msgs:
            @pl.when(ok)
            def _():
                m.start()

    def wait_recv_if(msgs):
        for _, ok, m, _ in msgs:
            @pl.when(ok)
            def _():
                m.wait_recv()

    def wait_send_if(msgs):
        for ok, _, m, _ in msgs:
            @pl.when(ok)
            def _():
                m.wait_send()

    def tile(ref, z, i, j):
        return ref[z, pl.ds(i * S, S), pl.ds(j * L, L)]

    for _, ok, _, buf in tin_msgs(0, 0) + floor_msgs(0):
        @pl.when(jnp.logical_not(ok))
        def _():
            buf[...] = jnp.zeros_like(buf)

    loads[0].wait()

    def pack_tin(z, carry):
        tlo_s[0, pl.ds(z, 1), :] = tin0[z, 0:1, :]
        thi_s[0, pl.ds(z, 1), :] = tin0[z, R - 1:R, :]
        return carry

    lax.fori_loop(0, Z, pack_tin, 0, unroll=4)

    peers = ty - 1
    for ok, _ in pairs:
        peers = peers + ok.astype(jnp.int32)
    pl.semaphore_wait(barrier, peers)

    t0, f0 = [tin_msgs(0, q) for q in range(NQ)], floor_msgs(0)
    t1 = [tin_msgs(1, q) for q in range(NQ)]
    p0, b0 = p_msgs(0, floor_h), b_msgs(0, tin_h)
    for m in p0 + b0:
        m.start()
    for q in range(NQ):
        start_if(t0[q])

    loads[1].wait()
    scalars[0].wait()
    c0, c1, c2 = cond[0] * 0.5, cond[1] * 0.5, cond[2] * 0.5
    NI, NJ = CX // S, CY // L

    def pack_cols(z, edge_lo, edge_hi, acc):
        lo_acc, hi_acc = acc
        here = lane == z
        lo_n = tuple(jnp.where(here, pltpu.roll(edge_lo[i], z, 1), lo_acc[i]) for i in range(NI))
        hi_n = tuple(jnp.where(here, pltpu.roll(edge_hi[i], z + 1, 1), hi_acc[i]) for i in range(NI))
        return lo_n, hi_n

    def zeros():
        zero = jnp.zeros((S, L), jnp.float32)
        return tuple(zero for _ in range(NI)), tuple(zero for _ in range(NI))

    def store_cols(slot, acc):
        for i in range(NI):
            clo_s[slot, pl.ds(i * S, S), :] = acc[0][i]
            chi_s[slot, pl.ds(i * S, S), :] = acc[1][i]

    def k_layer(z, acc):
        t = {}
        for i in range(NI):
            for j in range(NJ):
                m = tile(mat, z, i, j)
                v = jnp.where(m == 0, c0, jnp.where(m == 1, c1, c2))
                kh[z, pl.ds(i * S, S), pl.ds(j * L, L)] = v
                t[i, j] = v
        rlo_s[1, pl.ds(z, 1), :] = jnp.concatenate([t[0, j][0:1] for j in range(NJ)], 1)
        rhi_s[1, pl.ds(z, 1), :] = jnp.concatenate([t[NI - 1, j][S - 1:S] for j in range(NJ)], 1)
        return pack_cols(z, [t[i, 0] for i in range(NI)], [t[i, NJ - 1] for i in range(NI)], acc)

    store_cols(1, lax.fori_loop(0, ZF, k_layer, zeros(), unroll=4))
    loads[2].wait()

    def g_layer(z, acc):
        rlo_s[0, pl.ds(z, 1), :] = floor0[z, 0:1, :]
        rhi_s[0, pl.ds(z, 1), :] = floor0[z, CX - 1:CX, :]
        return pack_cols(z, [tile(floor0, z, i, 0) for i in range(NI)],
                         [tile(floor0, z, i, NJ - 1) for i in range(NI)], acc)

    store_cols(0, lax.fori_loop(0, ZF, g_layer, zeros(), unroll=4))
    start_if(f0)

    def floor_layer(first, src, dst, z, top, bottom):
        g, kxt, kyt = {}, {}, {}
        span = [(i, j) for i in range(NI) for j in range(NJ)]
        for i, j in span:
            g[i, j] = tile(src, z, i, j)
        if first:
            k = {ij: tile(kh, z, *ij) for ij in span}
            for i, j in span:
                r = pltpu.roll(k[i, j], S - 1, 0)
                if i < NI - 1:
                    v = k[i, j] + jnp.where(row_last, pltpu.roll(k[i + 1, j], S - 1, 0), r)
                else:
                    v = jnp.where(row_last, 0.0, k[i, j] + r)
                kxt[i, j] = v
                kx[z, pl.ds(i * S, S), pl.ds(j * L, L)] = v
                r = pltpu.roll(k[i, j], L - 1, 1)
                if j < NJ - 1:
                    v = k[i, j] + jnp.where(lane_last, pltpu.roll(k[i, j + 1], L - 1, 1), r)
                else:
                    v = jnp.where(lane_last, 0.0, k[i, j] + r)
                kyt[i, j] = v
                ky[z, pl.ds(i * S, S), pl.ds(j * L, L)] = v
                if bottom:
                    v = k[i, j]
                else:
                    v = k[i, j] + tile(kh, z + 1, i, j)
                kz[z, pl.ds(i * S, S), pl.ds(j * L, L)] = v
        else:
            for i, j in span:
                kxt[i, j] = tile(kx, z, i, j)
                kyt[i, j] = tile(ky, z, i, j)
        rx = {ij: pltpu.roll(g[ij], S - 1, 0) for ij in span}
        ry = {ij: pltpu.roll(g[ij], L - 1, 1) for ij in span}
        fx, fy, sx, sy = {}, {}, {}, {}
        for i, j in span:
            nx = rx[i, j] if i == NI - 1 else jnp.where(row_last, rx[i + 1, j], rx[i, j])
            ny = ry[i, j] if j == NJ - 1 else jnp.where(lane_last, ry[i, j + 1], ry[i, j])
            fx[i, j] = kxt[i, j] * (nx - g[i, j])
            fy[i, j] = kyt[i, j] * (ny - g[i, j])
            sx[i, j] = pltpu.roll(fx[i, j], 1, 0)
            sy[i, j] = pltpu.roll(fy[i, j], 1, 1)
        for i, j in span:
            px = jnp.where(row_first, sx[(i - 1) % NI, j], sx[i, j])
            py = jnp.where(lane_first, sy[i, (j - 1) % NJ], sy[i, j])
            if bottom:
                down = tile(kz, z, i, j) * g[i, j]
                new = g[i, j] - down
            else:
                new = g[i, j] + tile(kz, z, i, j) * (tile(src, z + 1, i, j) - g[i, j])
            if not top:
                new = new - tile(kz, z - 1, i, j) * (g[i, j] - tile(src, z - 1, i, j))
            new = new + ((fx[i, j] - px) + (fy[i, j] - py))
            dst[z, pl.ds(i * S, S), pl.ds(j * L, L)] = new

    def floor_sweep(first, src, dst):
        floor_layer(first, src, dst, 0, True, False)

        def body(z, carry):
            floor_layer(first, src, dst, z, False, False)
            return carry

        lax.fori_loop(1, ZF - 1, body, 0)
        floor_layer(first, src, dst, ZF - 1, False, True)

    def floor_edges(e, src, dst):
        g = 2 * e
        slot = 0 if e == 0 else 2
        rlo[slot] = (rlo_s[1] + rlo[1]) * (rlo[slot] - rlo_s[slot])
        rhi[slot] = (rhi_s[1] + rhi[1]) * (rhi[slot] - rhi_s[slot])
        clo[slot] = (clo_s[1] + clo[1]) * (clo[slot] - clo_s[slot])
        chi[slot] = (chi_s[1] + chi[1]) * (chi[slot] - chi_s[slot])
        dst[0] = dst[0] + HR * (bb[e] - src[0])

        def body(z, acc):
            row_lo, row_hi = rlo[slot, pl.ds(z, 1), :], rhi[slot, pl.ds(z, 1), :]
            t = {(i, j): tile(dst, z, i, j) for i in range(NI) for j in range(NJ)}
            for j in range(NJ):
                t[0, j] = t[0, j] + jnp.where(row_first, row_lo[:, j * L:j * L + L], 0.0)
                t[NI - 1, j] = t[NI - 1, j] + jnp.where(
                    row_last, row_hi[:, j * L:j * L + L], 0.0)
            for i in range(NI):
                low = pltpu.roll(clo[slot, pl.ds(i * S, S), :], lax.rem(L - z, L), 1)
                high = pltpu.roll(chi[slot, pl.ds(i * S, S), :], L - 1 - z, 1)
                t[i, 0] = t[i, 0] + jnp.where(lane_first, low, 0.0)
                t[i, NJ - 1] = t[i, NJ - 1] + jnp.where(lane_last, high, 0.0)
            for (i, j), v in t.items():
                dst[z, pl.ds(i * S, S), pl.ds(j * L, L)] = v
            if e == 1:
                return acc
            rlo_s[2, pl.ds(z, 1), :] = jnp.concatenate([t[0, j][0:1] for j in range(NJ)], 1)
            rhi_s[2, pl.ds(z, 1), :] = jnp.concatenate([t[NI - 1, j][S - 1:S] for j in range(NJ)], 1)
            return pack_cols(z, [t[i, 0] for i in range(NI)],
                             [t[i, NJ - 1] for i in range(NI)], acc)

        if e == 0:
            store_cols(2, lax.fori_loop(0, ZF, body, zeros(), unroll=4))
        else:
            lax.fori_loop(0, ZF, body, 0, unroll=4)

    NH, NK = R // S, NYW // L

    def tin_layer(e, src, dst, z, zu, zd, top):
        span = [(h, k) for h in range(NH) for k in range(NK)]
        s_x, s_y = speeds[0, z], speeds[1, z]
        keep = (1.0 - 6.0 * KT) - s_x - s_y
        u = {hk: tile(src, z, *hk) for hk in span}
        rd = {hk: pltpu.roll(u[hk], 1, 0) for hk in span}
        ru = {hk: pltpu.roll(u[hk], S - 1, 0) for hk in span}
        ld = {hk: pltpu.roll(u[hk], 1, 1) for hk in span}
        lu = {hk: pltpu.roll(u[hk], L - 1, 1) for hk in span}
        first_row, last_row = [], []
        before, after = tlo[e, pl.ds(z, 1), :], thi[e, pl.ds(z, 1), :]
        for h, k in span:
            v = u[h, k]
            below = before[:, k * L:k * L + L] if h == 0 else rd[h - 1, k]
            above = after[:, k * L:k * L + L] if h == NH - 1 else ru[h + 1, k]
            xm = jnp.where(row_first, below, rd[h, k])
            xp = jnp.where(row_last, above, ru[h, k])
            ym = jnp.where(lane_first, 0.0 if k == 0 else ld[h, k - 1], ld[h, k])
            yp = jnp.where(lane_last, 0.0 if k == NK - 1 else lu[h, k + 1], lu[h, k])
            f = tile(flow, z, h, k)
            total = ((xm + xp) + (ym + yp)) + (tile(src, zu, h, k) + tile(src, zd, h, k))
            new = keep * v + KT * total
            new = new + s_x * jnp.where((f & 1) == 0, xm, xp)
            new = new + s_y * jnp.where(f < 2, ym, yp)
            if top:
                new = new + HT * (pp[e, pl.ds(h * S, S), pl.ds(k * L, L)] - v)
            dst[z, pl.ds(h * S, S), pl.ds(k * L, L)] = new
            if h == 0:
                first_row.append(new[0:1])
            if h == NH - 1:
                last_row.append(new[S - 1:S])
        if e == 0:
            tlo_s[1, pl.ds(z, 1), :] = jnp.concatenate(first_row, 1)
            thi_s[1, pl.ds(z, 1), :] = jnp.concatenate(last_row, 1)

    def tin_sweep(e, src, dst, q):
        if q == 0:
            tin_layer(e, src, dst, 0, 1, 0, True)

        def body(z, carry):
            tin_layer(e, src, dst, z, jnp.minimum(z + 1, Z - 1), z - 1, False)
            return carry

        lax.fori_loop(max(1, q * ZQ), (q + 1) * ZQ, body, 0)

    floor_sweep(True, floor0, floor1)

    loads[3].wait()
    scalars[1].wait()
    for m in p0:
        m.wait_recv()
    own_p.wait()
    b1 = b_msgs(1, tin1)
    own_b1 = pltpu.make_async_copy(
        tin1.at[0, :, pl.ds(pl.multiple_of(c * CY, CY), CY)],
        bb.at[1, pl.ds(pl.multiple_of(c * R, R), R), :], load_sem.at[7])
    for q in range(NQ):
        wait_recv_if(t0[q])
        tin_sweep(0, tin0, tin1, q)
        start_if(t1[q])
        if q == 0:
            for m in b1:
                m.start()
            own_b1.start()

    wait_recv_if(f0)
    for m in b0:
        m.wait_recv()
    own_b.wait()
    wait_send_if(f0)
    floor_edges(0, floor0, floor1)
    f1, p1 = floor_msgs(1), p_msgs(1, floor1)
    for m in p1:
        m.start()
    start_if(f1)
    own_p1 = pltpu.make_async_copy(
        floor1.at[0, pl.ds(pl.multiple_of(c * R, R), R), :],
        pp.at[1, :, pl.ds(pl.multiple_of(c * CY, CY), CY)], load_sem.at[6])
    own_p1.start()

    floor_sweep(False, floor1, floor_o)
    for m in p1:
        m.wait_recv()
    own_p1.wait()
    for q in range(NQ):
        wait_recv_if(t1[q])
        tin_sweep(1, tin1, tin_o, q)

    wait_recv_if(f1)
    for m in b1:
        m.wait_recv()
    own_b1.wait()
    wait_send_if(f1)
    floor_edges(1, floor1, floor_o)

    for q in range(NQ):
        wait_send_if(t0[q])
        wait_send_if(t1[q])
    for m in p0 + b0 + p1 + b1:
        m.wait_send()


def local(n, ty, tin_temp, flow_code, speeds, floor_temp, material, conductivity):
    tin_shape = tin_temp.shape
    floor_shape = floor_temp.shape[1:]
    Z, R, NYW = tin_shape
    ZF, CX, CY = floor_shape
    f32, i32 = jnp.float32, jnp.int32
    V = pltpu.VMEM
    tin_v, floor_v = V(tin_shape, f32), V(floor_shape, f32)
    edge_t = V((2, Z, NYW), f32)
    edge_r = V((3, ZF, CY), f32)
    edge_c = V((3, CX, L), f32)
    tin_out, floor_out = pl.pallas_call(
        functools.partial(kernel, n, ty),
        out_shape=OUT(tin_shape, floor_shape),
        in_specs=[pl.BlockSpec(memory_space=m) for m in
                  (pltpu.HBM,) * 6],
        out_specs=[pl.BlockSpec(memory_space=pltpu.VMEM)] * 2,
        scratch_shapes=[
            pltpu.SMEM(speeds.shape, f32), pltpu.SMEM(conductivity.shape, f32),
            tin_v, V(tin_shape, i32), tin_v, floor_v, V(floor_shape, i32), floor_v,
            floor_v, floor_v, floor_v, floor_v,
            edge_t, edge_t, edge_t, edge_t,
            edge_r, edge_r, edge_r, edge_r,
            edge_c, edge_c, edge_c, edge_c,
            V((2, R, NYW), f32), V((2, CX, CY), f32),
            pltpu.SemaphoreType.DMA((10,)),
            pltpu.SemaphoreType.DMA((2, 12 + 2 * NQ)),
            pltpu.SemaphoreType.DMA((2, 12 + 2 * NQ)),
        ],
        compiler_params=pltpu.CompilerParams(
            collective_id=0, has_side_effects=True, vmem_limit_bytes=44 * 1024 * 1024),
        cost_estimate=pl.CostEstimate(flops=120_000_000, bytes_accessed=23_000_000, transcendentals=0),
    )(tin_temp, flow_code, speeds, floor_temp[0], material[0], conductivity)
    return tin_out, floor_out[None]


def OUT(tin_shape, floor_shape):
    return [pltpu.VMEM(tin_shape, jnp.float32), pltpu.VMEM(floor_shape, jnp.float32)]


def solution(mesh):
    n = mesh.shape["len"]
    split = ("grp", "len")
    placed = (P(None, split, None), P(None, split, None), P(),
              P(split, None, None, None), P(split, None, None, None), P())

    def whole(tin_temp, flow_code, speeds, floor_temp, material, conductivity):
        ty = tin_temp.shape[2] // floor_temp.shape[3]
        return jax.shard_map(
            functools.partial(local, n, ty),
            mesh=mesh,
            in_specs=placed,
            out_specs=(P(None, split, None), P(split, None, None, None)),
            check_vma=False,
        )(tin_temp, flow_code, speeds, floor_temp, material, conductivity)

    return whole
```

```python
import functools

import jax
import jax.numpy as jnp
from jax import lax
from jax.experimental import pallas as pl
from jax.experimental.pallas import tpu as pltpu
from jax.sharding import PartitionSpec as P

KT = 0.1
HT = 0.2
HR = 0.2
L = 128
NQ = 4
TU = 4
FU = 2
S = 8


def kernel(n, ty, tin_h, flow_h, speeds_h, floor_h, mat_h, cond_h,
           tin_o, floor_o,
           speeds, cond, tin0, flow, tin1, floor0, mat, floor1, kh, kx, ky, kz,
           tlo, thi, tlo_s, thi_s,
           rlo, rhi, rlo_s, rhi_s,
           clo, chi, clo_s, chi_s,
           pp, bb, load_sem, send_sem, recv_sem):
    Z, R, NYW = tin_h.shape
    ZF, CX, CY = floor_h.shape
    me = lax.axis_index("len")
    c = lax.rem(me, ty)
    base = me - c
    up_ok, dn_ok = me < n - 1, me > 0
    rup_ok, rdn_ok = me + ty < n, me >= ty
    cup_ok, cdn_ok = c < ty - 1, c > 0

    loads = [pltpu.make_async_copy(a, b, load_sem.at[i]) for i, (a, b) in enumerate(
        [(tin_h, tin0), (mat_h, mat), (floor_h, floor0), (flow_h, flow)])]
    scalars = [pltpu.make_async_copy(cond_h, cond, load_sem.at[8]),
               pltpu.make_async_copy(speeds_h, speeds, load_sem.at[9])]
    for ld in scalars:
        ld.start()
    for ld in loads:
        ld.start()

    barrier = pltpu.get_barrier_semaphore()

    def hello(target):
        pl.semaphore_signal(barrier, inc=1, device_id={"len": target},
                            device_id_type=pl.DeviceIdType.MESH)

    for d in range(1, ty):
        hello(base + lax.rem(c + d, ty))
    pairs = [(rup_ok, me + ty), (rdn_ok, me - ty),
             (jnp.logical_and(c == ty - 1, up_ok), me + 1),
             (jnp.logical_and(c == 0, dn_ok), me - 1)]
    for ok, target in pairs:
        @pl.when(ok)
        def _():
            hello(target)

    row = lax.broadcasted_iota(jnp.int32, (S, L), 0)
    lane = lax.broadcasted_iota(jnp.int32, (S, L), 1)
    row_first, row_last = row == 0, row == S - 1
    lane_first, lane_last = lane == 0, lane == L - 1

    own_p = pltpu.make_async_copy(
        floor_h.at[0, pl.ds(pl.multiple_of(c * R, R), R), :],
        pp.at[0, :, pl.ds(pl.multiple_of(c * CY, CY), CY)], load_sem.at[4])
    own_b = pltpu.make_async_copy(
        tin_h.at[0, :, pl.ds(pl.multiple_of(c * CY, CY), CY)],
        bb.at[0, pl.ds(pl.multiple_of(c * R, R), R), :], load_sem.at[5])
    own_p.start()
    own_b.start()

    def remote(e, slot, src, dst, target):
        return pltpu.make_async_remote_copy(
            src_ref=src, dst_ref=dst, send_sem=send_sem.at[e, slot],
            recv_sem=recv_sem.at[e, slot], device_id={"len": target},
            device_id_type=pl.DeviceIdType.MESH)

    ZQ = Z // NQ

    def tin_msgs(e, q):
        part = pl.ds(q * ZQ, ZQ)
        return [(up_ok, dn_ok, remote(e, 12 + q, thi_s.at[e, part], tlo.at[e, part], me + 1), tlo),
                (dn_ok, up_ok, remote(e, 12 + NQ + q, tlo_s.at[e, part], thi.at[e, part], me - 1), thi)]

    def floor_msgs(e):
        if e == 0:
            return [
                (rup_ok, rdn_ok, remote(0, 2, rhi_s.at[0:2], rlo.at[0:2], me + ty), rlo),
                (rdn_ok, rup_ok, remote(0, 3, rlo_s.at[0:2], rhi.at[0:2], me - ty), rhi),
                (cup_ok, cdn_ok, remote(0, 4, chi_s.at[0:2], clo.at[0:2], me + 1), clo),
                (cdn_ok, cup_ok, remote(0, 5, clo_s.at[0:2], chi.at[0:2], me - 1), chi)]
        return [
            (rup_ok, rdn_ok, remote(1, 2, rhi_s.at[2], rlo.at[2], me + ty), rlo),
            (rdn_ok, rup_ok, remote(1, 3, rlo_s.at[2], rhi.at[2], me - ty), rhi),
            (cup_ok, cdn_ok, remote(1, 4, chi_s.at[2], clo.at[2], me + 1), clo),
            (cdn_ok, cup_ok, remote(1, 5, clo_s.at[2], chi.at[2], me - 1), chi)]

    def p_msgs(e, field):
        out = []
        for d in range(1, ty):
            t = lax.rem(c + d, ty)
            out.append(remote(
                e, 5 + d, field.at[0, pl.ds(pl.multiple_of(t * R, R), R), :],
                pp.at[e, :, pl.ds(pl.multiple_of(c * CY, CY), CY)], base + t))
        return out

    def b_msgs(e, field):
        out = []
        for d in range(1, ty):
            t = lax.rem(c + d, ty)
            out.append(remote(
                e, 8 + d, field.at[0, :, pl.ds(pl.multiple_of(t * CY, CY), CY)],
                bb.at[e, pl.ds(pl.multiple_of(c * R, R), R), :], base + t))
        return out

    def start_if(msgs):
        for ok, _, m, _ in msgs:
            @pl.when(ok)
            def _():
                m.start()

    def wait_recv_if(msgs):
        for _, ok, m, _ in msgs:
            @pl.when(ok)
            def _():
                m.wait_recv()

    def wait_send_if(msgs):
        for ok, _, m, _ in msgs:
            @pl.when(ok)
            def _():
                m.wait_send()

    def tile(ref, z, i, j):
        return ref[z, pl.ds(i * S, S), pl.ds(j * L, L)]

    for _, ok, _, buf in tin_msgs(0, 0) + floor_msgs(0):
        @pl.when(jnp.logical_not(ok))
        def _():
            buf[...] = jnp.zeros_like(buf)

    loads[0].wait()

    def pack_tin(z, carry):
        tlo_s[0, pl.ds(z, 1), :] = tin0[z, 0:1, :]
        thi_s[0, pl.ds(z, 1), :] = tin0[z, R - 1:R, :]
        return carry

    lax.fori_loop(0, Z, pack_tin, 0, unroll=4)

    peers = ty - 1
    for ok, _ in pairs:
        peers = peers + ok.astype(jnp.int32)
    pl.semaphore_wait(barrier, peers)

    t0, f0 = [tin_msgs(0, q) for q in range(NQ)], floor_msgs(0)
    t1 = [tin_msgs(1, q) for q in range(NQ)]
    p0, b0 = p_msgs(0, floor_h), b_msgs(0, tin_h)
    for m in p0 + b0:
        m.start()
    for q in range(NQ):
        start_if(t0[q])

    loads[1].wait()
    scalars[0].wait()
    c0, c1, c2 = cond[0] * 0.5, cond[1] * 0.5, cond[2] * 0.5
    NI, NJ = CX // S, CY // L

    def pack_cols(z, edge_lo, edge_hi, acc):
        lo_acc, hi_acc = acc
        here = lane == z
        lo_n = tuple(jnp.where(here, pltpu.roll(edge_lo[i], z, 1), lo_acc[i]) for i in range(NI))
        hi_n = tuple(jnp.where(here, pltpu.roll(edge_hi[i], z + 1, 1), hi_acc[i]) for i in range(NI))
        return lo_n, hi_n

    def zeros():
        zero = jnp.zeros((S, L), jnp.float32)
        return tuple(zero for _ in range(NI)), tuple(zero for _ in range(NI))

    def store_cols(slot, acc):
        for i in range(NI):
            clo_s[slot, pl.ds(i * S, S), :] = acc[0][i]
            chi_s[slot, pl.ds(i * S, S), :] = acc[1][i]

    def k_layer(z, acc):
        t = {}
        for i in range(NI):
            for j in range(NJ):
                m = tile(mat, z, i, j)
                v = jnp.where(m == 0, c0, jnp.where(m == 1, c1, c2))
                kh[z, pl.ds(i * S, S), pl.ds(j * L, L)] = v
                t[i, j] = v
        rlo_s[1, pl.ds(z, 1), :] = jnp.concatenate([t[0, j][0:1] for j in range(NJ)], 1)
        rhi_s[1, pl.ds(z, 1), :] = jnp.concatenate([t[NI - 1, j][S - 1:S] for j in range(NJ)], 1)
        return pack_cols(z, [t[i, 0] for i in range(NI)], [t[i, NJ - 1] for i in range(NI)], acc)

    store_cols(1, lax.fori_loop(0, ZF, k_layer, zeros(), unroll=4))
    loads[2].wait()

    def g_layer(z, acc):
        rlo_s[0, pl.ds(z, 1), :] = floor0[z, 0:1, :]
        rhi_s[0, pl.ds(z, 1), :] = floor0[z, CX - 1:CX, :]
        return pack_cols(z, [tile(floor0, z, i, 0) for i in range(NI)],
                         [tile(floor0, z, i, NJ - 1) for i in range(NI)], acc)

    store_cols(0, lax.fori_loop(0, ZF, g_layer, zeros(), unroll=4))
    start_if(f0)

    def floor_layer(first, src, dst, z, top, bottom):
        def put(ref, i, j, v):
            ref[z, pl.ds(i * S, S), pl.ds(j * L, L)] = v
            return v

        def next_x(roll, i, j):
            if i == NI - 1:
                return roll(i, j)
            return jnp.where(row_last, roll(i + 1, j), roll(i, j))

        def next_y(roll, i, j):
            if j == NJ - 1:
                return roll(i, j)
            return jnp.where(lane_last, roll(i, j + 1), roll(i, j))

        def rolled(get, amount, dim):
            return functools.cache(lambda i, j: pltpu.roll(get(i, j), amount, dim))

        g = functools.cache(lambda i, j: tile(src, z, i, j))
        gx, gy = rolled(g, S - 1, 0), rolled(g, L - 1, 1)
        if first:
            k = functools.cache(lambda i, j: tile(kh, z, i, j))
            k_x, k_y = rolled(k, S - 1, 0), rolled(k, L - 1, 1)

            def face_x(i, j):
                v = k(i, j) + next_x(k_x, i, j)
                return put(kx, i, j, jnp.where(row_last, 0.0, v) if i == NI - 1 else v)

            def face_y(i, j):
                v = k(i, j) + next_y(k_y, i, j)
                return put(ky, i, j, jnp.where(lane_last, 0.0, v) if j == NJ - 1 else v)

            def face_z(i, j):
                return put(kz, i, j, k(i, j) if bottom else k(i, j) + tile(kh, z + 1, i, j))
        else:
            def face_x(i, j):
                return tile(kx, z, i, j)

            def face_y(i, j):
                return tile(ky, z, i, j)

            def face_z(i, j):
                return tile(kz, z, i, j)

        fx = functools.cache(lambda i, j: face_x(i, j) * (next_x(gx, i, j) - g(i, j)))
        fy = functools.cache(lambda i, j: face_y(i, j) * (next_y(gy, i, j) - g(i, j)))
        sx, sy = rolled(fx, 1, 0), rolled(fy, 1, 1)
        for i in range(NI):
            for j in range(NJ):
                px = jnp.where(row_first, sx(i - 1, j) if i else 0.0, sx(i, j))
                py = jnp.where(lane_first, sy(i, j - 1) if j else 0.0, sy(i, j))
                v = g(i, j)
                if bottom:
                    new = v - face_z(i, j) * v
                else:
                    new = v + face_z(i, j) * (tile(src, z + 1, i, j) - v)
                if not top:
                    new = new - tile(kz, z - 1, i, j) * (v - tile(src, z - 1, i, j))
                put(dst, i, j, new + ((fx(i, j) - px) + (fy(i, j) - py)))

    def floor_sweep(first, src, dst):
        floor_layer(first, src, dst, 0, True, False)

        def body(z, carry):
            floor_layer(first, src, dst, z, False, False)
            return carry

        lax.fori_loop(1, ZF - 1, body, 0, unroll=FU)
        floor_layer(first, src, dst, ZF - 1, False, True)

    def floor_edges(e, src, dst):
        g = 2 * e
        slot = 0 if e == 0 else 2
        rlo[slot] = (rlo_s[1] + rlo[1]) * (rlo[slot] - rlo_s[slot])
        rhi[slot] = (rhi_s[1] + rhi[1]) * (rhi[slot] - rhi_s[slot])
        clo[slot] = (clo_s[1] + clo[1]) * (clo[slot] - clo_s[slot])
        chi[slot] = (chi_s[1] + chi[1]) * (chi[slot] - chi_s[slot])
        dst[0] = dst[0] + HR * (bb[e] - src[0])

        def body(z, acc):
            row_lo, row_hi = rlo[slot, pl.ds(z, 1), :], rhi[slot, pl.ds(z, 1), :]
            t = {(i, j): tile(dst, z, i, j) for i in range(NI) for j in range(NJ)}
            for j in range(NJ):
                t[0, j] = t[0, j] + jnp.where(row_first, row_lo[:, j * L:j * L + L], 0.0)
                t[NI - 1, j] = t[NI - 1, j] + jnp.where(
                    row_last, row_hi[:, j * L:j * L + L], 0.0)
            for i in range(NI):
                low = pltpu.roll(clo[slot, pl.ds(i * S, S), :], lax.rem(L - z, L), 1)
                high = pltpu.roll(chi[slot, pl.ds(i * S, S), :], L - 1 - z, 1)
                t[i, 0] = t[i, 0] + jnp.where(lane_first, low, 0.0)
                t[i, NJ - 1] = t[i, NJ - 1] + jnp.where(lane_last, high, 0.0)
            for (i, j), v in t.items():
                dst[z, pl.ds(i * S, S), pl.ds(j * L, L)] = v
            if e == 1:
                return acc
            rlo_s[2, pl.ds(z, 1), :] = jnp.concatenate([t[0, j][0:1] for j in range(NJ)], 1)
            rhi_s[2, pl.ds(z, 1), :] = jnp.concatenate([t[NI - 1, j][S - 1:S] for j in range(NJ)], 1)
            return pack_cols(z, [t[i, 0] for i in range(NI)],
                             [t[i, NJ - 1] for i in range(NI)], acc)

        if e == 0:
            store_cols(2, lax.fori_loop(0, ZF, body, zeros(), unroll=4))
        else:
            lax.fori_loop(0, ZF, body, 0, unroll=4)

    NH, NK = R // S, NYW // L

    def tin_layer(e, src, dst, z, zu, zd, top):
        s_x, s_y = speeds[0, z], speeds[1, z]
        keep = (1.0 - 6.0 * KT) - s_x - s_y
        first_row, last_row = [], []
        before, after = tlo[e, pl.ds(z, 1), :], thi[e, pl.ds(z, 1), :]
        u = functools.cache(lambda h, k: tile(src, z, h, k))
        rd = functools.cache(lambda h, k: pltpu.roll(u(h, k), 1, 0))
        ru = functools.cache(lambda h, k: pltpu.roll(u(h, k), S - 1, 0))
        ld = functools.cache(lambda h, k: pltpu.roll(u(h, k), 1, 1))
        lu = functools.cache(lambda h, k: pltpu.roll(u(h, k), L - 1, 1))
        span = [(h, k) for k in range(NK) for h in range(NH)]
        for h, k in span:
            v = u(h, k)
            below = before[:, k * L:k * L + L] if h == 0 else rd(h - 1, k)
            above = after[:, k * L:k * L + L] if h == NH - 1 else ru(h + 1, k)
            xm = jnp.where(row_first, below, rd(h, k))
            xp = jnp.where(row_last, above, ru(h, k))
            ym = jnp.where(lane_first, 0.0 if k == 0 else ld(h, k - 1), ld(h, k))
            yp = jnp.where(lane_last, 0.0 if k == NK - 1 else lu(h, k + 1), lu(h, k))
            f = tile(flow, z, h, k)
            total = ((xm + xp) + (ym + yp)) + (tile(src, zu, h, k) + tile(src, zd, h, k))
            new = keep * v + KT * total
            new = new + s_x * jnp.where((f & 1) == 0, xm, xp)
            new = new + s_y * jnp.where(f < 2, ym, yp)
            if top:
                new = new + HT * (pp[e, pl.ds(h * S, S), pl.ds(k * L, L)] - v)
            dst[z, pl.ds(h * S, S), pl.ds(k * L, L)] = new
            if h == 0:
                first_row.append(new[0:1])
            if h == NH - 1:
                last_row.append(new[S - 1:S])
        if e == 0:
            tlo_s[1, pl.ds(z, 1), :] = jnp.concatenate(first_row, 1)
            thi_s[1, pl.ds(z, 1), :] = jnp.concatenate(last_row, 1)

    def tin_sweep(e, src, dst, q):
        if q == 0:
            tin_layer(e, src, dst, 0, 1, 0, True)

        def body(z, carry):
            tin_layer(e, src, dst, z, jnp.minimum(z + 1, Z - 1), z - 1, False)
            return carry

        lax.fori_loop(max(1, q * ZQ), (q + 1) * ZQ, body, 0, unroll=TU)

    floor_sweep(True, floor0, floor1)

    loads[3].wait()
    scalars[1].wait()
    for m in p0:
        m.wait_recv()
    own_p.wait()
    b1 = b_msgs(1, tin1)
    own_b1 = pltpu.make_async_copy(
        tin1.at[0, :, pl.ds(pl.multiple_of(c * CY, CY), CY)],
        bb.at[1, pl.ds(pl.multiple_of(c * R, R), R), :], load_sem.at[7])
    for q in range(NQ):
        wait_recv_if(t0[q])
        tin_sweep(0, tin0, tin1, q)
        start_if(t1[q])
        if q == 0:
            for m in b1:
                m.start()
            own_b1.start()

    wait_recv_if(f0)
    for m in b0:
        m.wait_recv()
    own_b.wait()
    wait_send_if(f0)
    floor_edges(0, floor0, floor1)
    f1, p1 = floor_msgs(1), p_msgs(1, floor1)
    for m in p1:
        m.start()
    start_if(f1)
    own_p1 = pltpu.make_async_copy(
        floor1.at[0, pl.ds(pl.multiple_of(c * R, R), R), :],
        pp.at[1, :, pl.ds(pl.multiple_of(c * CY, CY), CY)], load_sem.at[6])
    own_p1.start()

    floor_sweep(False, floor1, floor_o)
    for m in p1:
        m.wait_recv()
    own_p1.wait()
    for q in range(NQ):
        wait_recv_if(t1[q])
        tin_sweep(1, tin1, tin_o, q)

    wait_recv_if(f1)
    for m in b1:
        m.wait_recv()
    own_b1.wait()
    wait_send_if(f1)
    floor_edges(1, floor1, floor_o)

    for q in range(NQ):
        wait_send_if(t0[q])
        wait_send_if(t1[q])
    for m in p0 + b0 + p1 + b1:
        m.wait_send()


def local(n, ty, tin_temp, flow_code, speeds, floor_temp, material, conductivity):
    tin_shape = tin_temp.shape
    floor_shape = floor_temp.shape[1:]
    Z, R, NYW = tin_shape
    ZF, CX, CY = floor_shape
    f32, i32 = jnp.float32, jnp.int32
    V = pltpu.VMEM
    tin_v, floor_v = V(tin_shape, f32), V(floor_shape, f32)
    edge_t = V((2, Z, NYW), f32)
    edge_r = V((3, ZF, CY), f32)
    edge_c = V((3, CX, L), f32)
    tin_out, floor_out = pl.pallas_call(
        functools.partial(kernel, n, ty),
        out_shape=OUT(tin_shape, floor_shape),
        in_specs=[pl.BlockSpec(memory_space=m) for m in
                  (pltpu.HBM,) * 6],
        out_specs=[pl.BlockSpec(memory_space=pltpu.VMEM)] * 2,
        scratch_shapes=[
            pltpu.SMEM(speeds.shape, f32), pltpu.SMEM(conductivity.shape, f32),
            tin_v, V(tin_shape, i32), tin_v, floor_v, V(floor_shape, i32), floor_v,
            floor_v, floor_v, floor_v, floor_v,
            edge_t, edge_t, edge_t, edge_t,
            edge_r, edge_r, edge_r, edge_r,
            edge_c, edge_c, edge_c, edge_c,
            V((2, R, NYW), f32), V((2, CX, CY), f32),
            pltpu.SemaphoreType.DMA((10,)),
            pltpu.SemaphoreType.DMA((2, 12 + 2 * NQ)),
            pltpu.SemaphoreType.DMA((2, 12 + 2 * NQ)),
        ],
        compiler_params=pltpu.CompilerParams(
            collective_id=0, has_side_effects=True, vmem_limit_bytes=44 * 1024 * 1024),
        cost_estimate=pl.CostEstimate(flops=120_000_000, bytes_accessed=23_000_000, transcendentals=0),
    )(tin_temp, flow_code, pltpu.with_memory_space_constraint(speeds, pltpu.HBM), floor_temp[0],
      material[0], pltpu.with_memory_space_constraint(conductivity, pltpu.HBM))
    return tin_out, floor_out[None]


def OUT(tin_shape, floor_shape):
    return [pltpu.VMEM(tin_shape, jnp.float32), pltpu.VMEM(floor_shape, jnp.float32)]


def solution(mesh):
    n = mesh.shape["len"]
    split = ("grp", "len")
    placed = (P(None, split, None), P(None, split, None), P(),
              P(split, None, None, None), P(split, None, None, None), P())

    def whole(tin_temp, flow_code, speeds, floor_temp, material, conductivity):
        ty = tin_temp.shape[2] // floor_temp.shape[3]
        return jax.shard_map(
            functools.partial(local, n, ty),
            mesh=mesh,
            in_specs=placed,
            out_specs=(P(None, split, None), P(split, None, None, None)),
            check_vma=False,
        )(tin_temp, flow_code, speeds, floor_temp, material, conductivity)

    return whole
```

```python
import functools

import jax
import jax.numpy as jnp
from jax import lax
from jax.experimental import pallas as pl
from jax.experimental.pallas import tpu as pltpu
from jax.sharding import PartitionSpec as P

KT = 0.1
HT = 0.2
HR = 0.2
L = 128
NQ = 4
TU = 4
FU = 3
S = 8


def kernel(n, ty, tin_h, flow_h, speeds_h, floor_h, mat_h, cond_h,
           tin_o, floor_o,
           speeds, cond, tin0, flow, tin1, floor0, mat, floor1, kh, kx, ky, kz,
           tlo, thi, tlo_s, thi_s,
           rlo, rhi, rlo_s, rhi_s,
           clo, chi, clo_s, chi_s,
           pp, bb, load_sem, send_sem, recv_sem):
    Z, R, NYW = tin_h.shape
    ZF, CX, CY = floor_h.shape
    me = lax.axis_index("len")
    c = lax.rem(me, ty)
    base = me - c
    up_ok, dn_ok = me < n - 1, me > 0
    rup_ok, rdn_ok = me + ty < n, me >= ty
    cup_ok, cdn_ok = c < ty - 1, c > 0

    loads = [pltpu.make_async_copy(a, b, load_sem.at[i]) for i, (a, b) in enumerate(
        [(tin_h, tin0), (mat_h, mat), (floor_h, floor0), (flow_h, flow)])]
    scalars = [pltpu.make_async_copy(cond_h, cond, load_sem.at[8]),
               pltpu.make_async_copy(speeds_h, speeds, load_sem.at[9])]
    for ld in scalars:
        ld.start()
    for ld in loads:
        ld.start()

    barrier = pltpu.get_barrier_semaphore()

    def hello(target):
        pl.semaphore_signal(barrier, inc=1, device_id={"len": target},
                            device_id_type=pl.DeviceIdType.MESH)

    for d in range(1, ty):
        hello(base + lax.rem(c + d, ty))
    pairs = [(rup_ok, me + ty), (rdn_ok, me - ty),
             (jnp.logical_and(c == ty - 1, up_ok), me + 1),
             (jnp.logical_and(c == 0, dn_ok), me - 1)]
    for ok, target in pairs:
        @pl.when(ok)
        def _():
            hello(target)

    row = lax.broadcasted_iota(jnp.int32, (S, L), 0)
    lane = lax.broadcasted_iota(jnp.int32, (S, L), 1)
    row_first, row_last = row == 0, row == S - 1
    lane_first, lane_last = lane == 0, lane == L - 1

    own_p = pltpu.make_async_copy(
        floor_h.at[0, pl.ds(pl.multiple_of(c * R, R), R), :],
        pp.at[0, :, pl.ds(pl.multiple_of(c * CY, CY), CY)], load_sem.at[4])
    own_b = pltpu.make_async_copy(
        tin_h.at[0, :, pl.ds(pl.multiple_of(c * CY, CY), CY)],
        bb.at[0, pl.ds(pl.multiple_of(c * R, R), R), :], load_sem.at[5])
    own_p.start()
    own_b.start()

    def remote(e, slot, src, dst, target):
        return pltpu.make_async_remote_copy(
            src_ref=src, dst_ref=dst, send_sem=send_sem.at[e, slot],
            recv_sem=recv_sem.at[e, slot], device_id={"len": target},
            device_id_type=pl.DeviceIdType.MESH)

    ZQ = Z // NQ

    def tin_msgs(e, q):
        part = pl.ds(q * ZQ, ZQ)
        return [(up_ok, dn_ok, remote(e, 12 + q, thi_s.at[e, part], tlo.at[e, part], me + 1), tlo),
                (dn_ok, up_ok, remote(e, 12 + NQ + q, tlo_s.at[e, part], thi.at[e, part], me - 1), thi)]

    def floor_msgs(e):
        if e == 0:
            return [
                (rup_ok, rdn_ok, remote(0, 2, rhi_s.at[0:2], rlo.at[0:2], me + ty), rlo),
                (rdn_ok, rup_ok, remote(0, 3, rlo_s.at[0:2], rhi.at[0:2], me - ty), rhi),
                (cup_ok, cdn_ok, remote(0, 4, chi_s.at[0:2], clo.at[0:2], me + 1), clo),
                (cdn_ok, cup_ok, remote(0, 5, clo_s.at[0:2], chi.at[0:2], me - 1), chi)]
        return [
            (rup_ok, rdn_ok, remote(1, 2, rhi_s.at[2], rlo.at[2], me + ty), rlo),
            (rdn_ok, rup_ok, remote(1, 3, rlo_s.at[2], rhi.at[2], me - ty), rhi),
            (cup_ok, cdn_ok, remote(1, 4, chi_s.at[2], clo.at[2], me + 1), clo),
            (cdn_ok, cup_ok, remote(1, 5, clo_s.at[2], chi.at[2], me - 1), chi)]

    def p_msgs(e, field):
        out = []
        for d in range(1, ty):
            t = lax.rem(c + d, ty)
            out.append(remote(
                e, 5 + d, field.at[0, pl.ds(pl.multiple_of(t * R, R), R), :],
                pp.at[e, :, pl.ds(pl.multiple_of(c * CY, CY), CY)], base + t))
        return out

    def b_msgs(e, field):
        out = []
        for d in range(1, ty):
            t = lax.rem(c + d, ty)
            out.append(remote(
                e, 8 + d, field.at[0, :, pl.ds(pl.multiple_of(t * CY, CY), CY)],
                bb.at[e, pl.ds(pl.multiple_of(c * R, R), R), :], base + t))
        return out

    def start_if(msgs):
        for ok, _, m, _ in msgs:
            @pl.when(ok)
            def _():
                m.start()

    def wait_recv_if(msgs):
        for _, ok, m, _ in msgs:
            @pl.when(ok)
            def _():
                m.wait_recv()

    def wait_send_if(msgs):
        for ok, _, m, _ in msgs:
            @pl.when(ok)
            def _():
                m.wait_send()

    def tile(ref, z, i, j):
        return ref[z, pl.ds(i * S, S), pl.ds(j * L, L)]

    for _, ok, _, buf in tin_msgs(0, 0) + floor_msgs(0):
        @pl.when(jnp.logical_not(ok))
        def _():
            buf[...] = jnp.zeros_like(buf)

    loads[0].wait()

    def pack_tin(z, carry):
        tlo_s[0, pl.ds(z, 1), :] = tin0[z, 0:1, :]
        thi_s[0, pl.ds(z, 1), :] = tin0[z, R - 1:R, :]
        return carry

    lax.fori_loop(0, Z, pack_tin, 0, unroll=8)

    peers = ty - 1
    for ok, _ in pairs:
        peers = peers + ok.astype(jnp.int32)
    pl.semaphore_wait(barrier, peers)

    t0, f0 = [tin_msgs(0, q) for q in range(NQ)], floor_msgs(0)
    t1 = [tin_msgs(1, q) for q in range(NQ)]
    p0, b0 = p_msgs(0, floor_h), b_msgs(0, tin_h)
    for m in p0 + b0:
        m.start()
    for q in range(NQ):
        start_if(t0[q])

    loads[1].wait()
    scalars[0].wait()
    c0, c1, c2 = cond[0] * 0.5, cond[1] * 0.5, cond[2] * 0.5
    NI, NJ = CX // S, CY // L

    def pack_cols(z, edge_lo, edge_hi, acc):
        lo_acc, hi_acc = acc
        here = lane == z
        lo_n = tuple(jnp.where(here, pltpu.roll(edge_lo[i], z, 1), lo_acc[i]) for i in range(NI))
        hi_n = tuple(jnp.where(here, pltpu.roll(edge_hi[i], z + 1, 1), hi_acc[i]) for i in range(NI))
        return lo_n, hi_n

    def zeros():
        zero = jnp.zeros((S, L), jnp.float32)
        return tuple(zero for _ in range(NI)), tuple(zero for _ in range(NI))

    def store_cols(slot, acc):
        for i in range(NI):
            clo_s[slot, pl.ds(i * S, S), :] = acc[0][i]
            chi_s[slot, pl.ds(i * S, S), :] = acc[1][i]

    def k_layer(z, acc):
        t = {}
        for i in range(NI):
            for j in range(NJ):
                m = tile(mat, z, i, j)
                v = jnp.where(m == 0, c0, jnp.where(m == 1, c1, c2))
                kh[z, pl.ds(i * S, S), pl.ds(j * L, L)] = v
                t[i, j] = v
        rlo_s[1, pl.ds(z, 1), :] = jnp.concatenate([t[0, j][0:1] for j in range(NJ)], 1)
        rhi_s[1, pl.ds(z, 1), :] = jnp.concatenate([t[NI - 1, j][S - 1:S] for j in range(NJ)], 1)
        return pack_cols(z, [t[i, 0] for i in range(NI)], [t[i, NJ - 1] for i in range(NI)], acc)

    store_cols(1, lax.fori_loop(0, ZF, k_layer, zeros(), unroll=8))
    loads[2].wait()

    def g_layer(z, acc):
        rlo_s[0, pl.ds(z, 1), :] = floor0[z, 0:1, :]
        rhi_s[0, pl.ds(z, 1), :] = floor0[z, CX - 1:CX, :]
        return pack_cols(z, [tile(floor0, z, i, 0) for i in range(NI)],
                         [tile(floor0, z, i, NJ - 1) for i in range(NI)], acc)

    store_cols(0, lax.fori_loop(0, ZF, g_layer, zeros(), unroll=8))
    start_if(f0)

    def floor_layer(first, src, dst, z, top, bottom):
        def put(ref, i, j, v):
            ref[z, pl.ds(i * S, S), pl.ds(j * L, L)] = v
            return v

        def next_x(roll, i, j):
            if i == NI - 1:
                return roll(i, j)
            return jnp.where(row_last, roll(i + 1, j), roll(i, j))

        def next_y(roll, i, j):
            if j == NJ - 1:
                return roll(i, j)
            return jnp.where(lane_last, roll(i, j + 1), roll(i, j))

        def rolled(get, amount, dim):
            return functools.cache(lambda i, j: pltpu.roll(get(i, j), amount, dim))

        g = functools.cache(lambda i, j: tile(src, z, i, j))
        gx, gy = rolled(g, S - 1, 0), rolled(g, L - 1, 1)
        if first:
            k = functools.cache(lambda i, j: tile(kh, z, i, j))
            k_x, k_y = rolled(k, S - 1, 0), rolled(k, L - 1, 1)

            def face_x(i, j):
                v = k(i, j) + next_x(k_x, i, j)
                return put(kx, i, j, jnp.where(row_last, 0.0, v) if i == NI - 1 else v)

            def face_y(i, j):
                v = k(i, j) + next_y(k_y, i, j)
                return put(ky, i, j, jnp.where(lane_last, 0.0, v) if j == NJ - 1 else v)

            def face_z(i, j):
                return put(kz, i, j, k(i, j) if bottom else k(i, j) + tile(kh, z + 1, i, j))
        else:
            def face_x(i, j):
                return tile(kx, z, i, j)

            def face_y(i, j):
                return tile(ky, z, i, j)

            def face_z(i, j):
                return tile(kz, z, i, j)

        fx = functools.cache(lambda i, j: face_x(i, j) * (next_x(gx, i, j) - g(i, j)))
        fy = functools.cache(lambda i, j: face_y(i, j) * (next_y(gy, i, j) - g(i, j)))
        sx, sy = rolled(fx, 1, 0), rolled(fy, 1, 1)
        for i in range(NI):
            for j in range(NJ):
                px = jnp.where(row_first, sx(i - 1, j) if i else 0.0, sx(i, j))
                py = jnp.where(lane_first, sy(i, j - 1) if j else 0.0, sy(i, j))
                v = g(i, j)
                if bottom:
                    new = v - face_z(i, j) * v
                else:
                    new = v + face_z(i, j) * (tile(src, z + 1, i, j) - v)
                if not top:
                    new = new - tile(kz, z - 1, i, j) * (v - tile(src, z - 1, i, j))
                put(dst, i, j, new + ((fx(i, j) - px) + (fy(i, j) - py)))

    def floor_sweep(first, src, dst):
        floor_layer(first, src, dst, 0, True, False)

        def body(z, carry):
            floor_layer(first, src, dst, z, False, False)
            return carry

        lax.fori_loop(1, ZF - 1, body, 0, unroll=FU)
        floor_layer(first, src, dst, ZF - 1, False, True)

    def floor_edges(e, src, dst):
        g = 2 * e
        slot = 0 if e == 0 else 2
        rlo[slot] = (rlo_s[1] + rlo[1]) * (rlo[slot] - rlo_s[slot])
        rhi[slot] = (rhi_s[1] + rhi[1]) * (rhi[slot] - rhi_s[slot])
        clo[slot] = (clo_s[1] + clo[1]) * (clo[slot] - clo_s[slot])
        chi[slot] = (chi_s[1] + chi[1]) * (chi[slot] - chi_s[slot])
        dst[0] = dst[0] + HR * (bb[e] - src[0])

        def body(z, acc):
            row_lo, row_hi = rlo[slot, pl.ds(z, 1), :], rhi[slot, pl.ds(z, 1), :]
            t = {(i, j): tile(dst, z, i, j) for i in range(NI) for j in range(NJ)}
            for j in range(NJ):
                t[0, j] = t[0, j] + jnp.where(row_first, row_lo[:, j * L:j * L + L], 0.0)
                t[NI - 1, j] = t[NI - 1, j] + jnp.where(
                    row_last, row_hi[:, j * L:j * L + L], 0.0)
            for i in range(NI):
                low = pltpu.roll(clo[slot, pl.ds(i * S, S), :], lax.rem(L - z, L), 1)
                high = pltpu.roll(chi[slot, pl.ds(i * S, S), :], L - 1 - z, 1)
                t[i, 0] = t[i, 0] + jnp.where(lane_first, low, 0.0)
                t[i, NJ - 1] = t[i, NJ - 1] + jnp.where(lane_last, high, 0.0)
            for (i, j), v in t.items():
                dst[z, pl.ds(i * S, S), pl.ds(j * L, L)] = v
            if e == 1:
                return acc
            rlo_s[2, pl.ds(z, 1), :] = jnp.concatenate([t[0, j][0:1] for j in range(NJ)], 1)
            rhi_s[2, pl.ds(z, 1), :] = jnp.concatenate([t[NI - 1, j][S - 1:S] for j in range(NJ)], 1)
            return pack_cols(z, [t[i, 0] for i in range(NI)],
                             [t[i, NJ - 1] for i in range(NI)], acc)

        if e == 0:
            store_cols(2, lax.fori_loop(0, ZF, body, zeros(), unroll=8))
        else:
            lax.fori_loop(0, ZF, body, 0, unroll=8)

    NH, NK = R // S, NYW // L

    def tin_layer(e, src, dst, z, zu, zd, top):
        s_x, s_y = speeds[0, z], speeds[1, z]
        keep = (1.0 - 6.0 * KT) - s_x - s_y
        first_row, last_row = [], []
        before, after = tlo[e, pl.ds(z, 1), :], thi[e, pl.ds(z, 1), :]
        u = functools.cache(lambda h, k: tile(src, z, h, k))
        rd = functools.cache(lambda h, k: pltpu.roll(u(h, k), 1, 0))
        ru = functools.cache(lambda h, k: pltpu.roll(u(h, k), S - 1, 0))
        ld = functools.cache(lambda h, k: pltpu.roll(u(h, k), 1, 1))
        lu = functools.cache(lambda h, k: pltpu.roll(u(h, k), L - 1, 1))
        span = [(h, k) for k in range(NK) for h in range(NH)]
        for h, k in span:
            v = u(h, k)
            below = before[:, k * L:k * L + L] if h == 0 else rd(h - 1, k)
            above = after[:, k * L:k * L + L] if h == NH - 1 else ru(h + 1, k)
            xm = jnp.where(row_first, below, rd(h, k))
            xp = jnp.where(row_last, above, ru(h, k))
            ym = jnp.where(lane_first, 0.0 if k == 0 else ld(h, k - 1), ld(h, k))
            yp = jnp.where(lane_last, 0.0 if k == NK - 1 else lu(h, k + 1), lu(h, k))
            f = tile(flow, z, h, k)
            total = ((xm + xp) + (ym + yp)) + (tile(src, zu, h, k) + tile(src, zd, h, k))
            new = keep * v + KT * total
            new = new + s_x * jnp.where((f & 1) == 0, xm, xp)
            new = new + s_y * jnp.where(f < 2, ym, yp)
            if top:
                new = new + HT * (pp[e, pl.ds(h * S, S), pl.ds(k * L, L)] - v)
            dst[z, pl.ds(h * S, S), pl.ds(k * L, L)] = new
            if h == 0:
                first_row.append(new[0:1])
            if h == NH - 1:
                last_row.append(new[S - 1:S])
        if e == 0:
            tlo_s[1, pl.ds(z, 1), :] = jnp.concatenate(first_row, 1)
            thi_s[1, pl.ds(z, 1), :] = jnp.concatenate(last_row, 1)

    def tin_sweep(e, src, dst, q):
        if q == 0:
            tin_layer(e, src, dst, 0, 1, 0, True)

        def body(z, carry):
            tin_layer(e, src, dst, z, jnp.minimum(z + 1, Z - 1), z - 1, False)
            return carry

        lax.fori_loop(max(1, q * ZQ), (q + 1) * ZQ, body, 0, unroll=TU)

    floor_sweep(True, floor0, floor1)

    loads[3].wait()
    scalars[1].wait()
    for m in p0:
        m.wait_recv()
    own_p.wait()
    b1 = b_msgs(1, tin1)
    own_b1 = pltpu.make_async_copy(
        tin1.at[0, :, pl.ds(pl.multiple_of(c * CY, CY), CY)],
        bb.at[1, pl.ds(pl.multiple_of(c * R, R), R), :], load_sem.at[7])
    for q in range(NQ):
        wait_recv_if(t0[q])
        tin_sweep(0, tin0, tin1, q)
        start_if(t1[q])
        if q == 0:
            for m in b1:
                m.start()
            own_b1.start()

    wait_recv_if(f0)
    for m in b0:
        m.wait_recv()
    own_b.wait()
    wait_send_if(f0)
    floor_edges(0, floor0, floor1)
    f1, p1 = floor_msgs(1), p_msgs(1, floor1)
    for m in p1:
        m.start()
    start_if(f1)
    own_p1 = pltpu.make_async_copy(
        floor1.at[0, pl.ds(pl.multiple_of(c * R, R), R), :],
        pp.at[1, :, pl.ds(pl.multiple_of(c * CY, CY), CY)], load_sem.at[6])
    own_p1.start()

    floor_sweep(False, floor1, floor_o)
    for m in p1:
        m.wait_recv()
    own_p1.wait()
    for q in range(NQ):
        wait_recv_if(t1[q])
        tin_sweep(1, tin1, tin_o, q)

    wait_recv_if(f1)
    for m in b1:
        m.wait_recv()
    own_b1.wait()
    wait_send_if(f1)
    floor_edges(1, floor1, floor_o)

    for q in range(NQ):
        wait_send_if(t0[q])
        wait_send_if(t1[q])
    for m in p0 + b0 + p1 + b1:
        m.wait_send()


def local(n, ty, tin_temp, flow_code, speeds, floor_temp, material, conductivity):
    tin_shape = tin_temp.shape
    floor_shape = floor_temp.shape[1:]
    Z, R, NYW = tin_shape
    ZF, CX, CY = floor_shape
    f32, i32 = jnp.float32, jnp.int32
    V = pltpu.VMEM
    tin_v, floor_v = V(tin_shape, f32), V(floor_shape, f32)
    edge_t = V((2, Z, NYW), f32)
    edge_r = V((3, ZF, CY), f32)
    edge_c = V((3, CX, L), f32)
    tin_out, floor_out = pl.pallas_call(
        functools.partial(kernel, n, ty),
        out_shape=OUT(tin_shape, floor_shape),
        in_specs=[pl.BlockSpec(memory_space=m) for m in
                  (pltpu.HBM,) * 6],
        out_specs=[pl.BlockSpec(memory_space=pltpu.VMEM)] * 2,
        scratch_shapes=[
            pltpu.SMEM(speeds.shape, f32), pltpu.SMEM(conductivity.shape, f32),
            tin_v, V(tin_shape, i32), tin_v, floor_v, V(floor_shape, i32), floor_v,
            floor_v, floor_v, floor_v, floor_v,
            edge_t, edge_t, edge_t, edge_t,
            edge_r, edge_r, edge_r, edge_r,
            edge_c, edge_c, edge_c, edge_c,
            V((2, R, NYW), f32), V((2, CX, CY), f32),
            pltpu.SemaphoreType.DMA((10,)),
            pltpu.SemaphoreType.DMA((2, 12 + 2 * NQ)),
            pltpu.SemaphoreType.DMA((2, 12 + 2 * NQ)),
        ],
        compiler_params=pltpu.CompilerParams(
            collective_id=0, has_side_effects=True, vmem_limit_bytes=44 * 1024 * 1024),
        cost_estimate=pl.CostEstimate(flops=120_000_000, bytes_accessed=23_000_000, transcendentals=0),
    )(tin_temp, flow_code, pltpu.with_memory_space_constraint(speeds, pltpu.HBM), floor_temp[0],
      material[0], pltpu.with_memory_space_constraint(conductivity, pltpu.HBM))
    return tin_out, floor_out[None]


def OUT(tin_shape, floor_shape):
    return [pltpu.VMEM(tin_shape, jnp.float32), pltpu.VMEM(floor_shape, jnp.float32)]


def solution(mesh):
    n = mesh.shape["len"]
    split = ("grp", "len")
    placed = (P(None, split, None), P(None, split, None), P(),
              P(split, None, None, None), P(split, None, None, None), P())

    def whole(tin_temp, flow_code, speeds, floor_temp, material, conductivity):
        ty = tin_temp.shape[2] // floor_temp.shape[3]
        return jax.shard_map(
            functools.partial(local, n, ty),
            mesh=mesh,
            in_specs=placed,
            out_specs=(P(None, split, None), P(split, None, None, None)),
            check_vma=False,
        )(tin_temp, flow_code, speeds, floor_temp, material, conductivity)

    return whole
```
